256 devices in a mesh: view: 8 (over z), head: 32 (over y, x, core).
Axes of the slice: x: 4, y: 4, z: 8, core: 2. Of those that a mesh axis runs over, the one named last changes fastest.
Arguments:
- query_tokens: bfloat16 [32768, 4096], P(('view', 'head')), may hold values from -5 to 5
- key_tokens: bfloat16 [32768, 4096], P(('view', 'head')), may hold values from -5 to 5
- value_tokens: bfloat16 [32768, 4096], P(('view', 'head')), may hold values from -6 to 6
- cotangent: bfloat16 [32768, 4096], P(('view', 'head')), may hold values from -6 to 6
- neighbors: int32 [64, 2], replicated, may hold values from 0 to 63, as said below
- view_slot: int32 [64], replicated, may hold values from 0 to 63, as said below
Outputs:
- attended: bfloat16 [32768, 4096], P(('view', 'head'))
- query_grads: bfloat16 [32768, 4096], P(('view', 'head'))
- key_grads: bfloat16 [32768, 4096], P(('view', 'head'))
- value_grads: bfloat16 [32768, 4096], P(('view', 'head'))
The draws below stay inside these ranges and needn't reach their ends.
Inputs may be any that keep to these rules, and one draw needn't show every extreme that they name: `view_slot`: A permutation of the views. `neighbors`: entry 0 of row v is v. Every other entry either repeats v or names a distinct view whose slot lies in another group than v's. The views that the views of one group name in any single other group are at most 1, and some group names exactly 1 in every other group; the views of one group named by views of other groups are exactly 2 for every group.
All inputs are finite; a program needn't handle non-finite values.
Results may differ from the reference program's by a relative error of at most 0.023.
Values may be sent and summed in bfloat16 or wider, within the bound.
A program may use at most 128 MiB of HBM per device.

```python
import math
import jax
import jax.numpy as jnp
from jax import lax

HEADS = 32
HD = 128
L = 512
V_G = 8
EXP = 2
CAP = 1
VIEWS = 64
TOKENS = 32768
NB = 2
N_VIEW = 8


def adjacency_tables(key):
    subkeys = jax.random.split(key, 7)
    groups = N_VIEW
    per_group = V_G
    view_total = VIEWS
    cover_count = (EXP + CAP - 1) // CAP
    local_scores = jax.random.randint(subkeys[0], (groups, per_group), 0, 1 << 20) * per_group + jnp.arange(per_group)[None, :]
    local_order = jnp.argsort(local_scores, axis=1, stable=True).astype(jnp.int32)
    export_list = local_order[:, :EXP]
    counts = jax.random.randint(subkeys[1], (groups, groups), 0, CAP + 1)
    full_dest = jax.random.randint(subkeys[2], (), 0, groups)
    shift_cover = jax.random.randint(subkeys[3], (groups,), 0, groups - 1)
    offsets = jax.random.randint(subkeys[4], (groups, groups), 0, EXP)
    dest_group = jnp.arange(groups)[:, None]
    source_group = jnp.arange(groups)[None, :]
    relative = (dest_group - source_group - 1) % groups
    cover_rank = (relative - shift_cover[None, :]) % (groups - 1)
    forced = (relative < groups - 1) & (cover_rank < cover_count)
    counts = jnp.where(forced | (dest_group == full_dest), CAP, counts)
    counts = jnp.where(dest_group == source_group, 0, counts)
    offsets = jnp.where(forced, cover_rank * CAP % EXP, offsets)
    slot_step = jnp.arange(CAP)
    position = (offsets[:, :, None] + slot_step[None, None, :]) % EXP
    live_slot = slot_step[None, None, :] < counts[:, :, None]
    local_view = jnp.take_along_axis(jnp.broadcast_to(export_list[None, :, :], (groups, groups, EXP)), position, axis=2)
    source_slot = (source_group[:, :, None] * per_group + local_view).reshape(groups, groups * CAP)
    live_flat = live_slot.reshape(groups, groups * CAP)
    rank_table = jnp.cumsum(live_flat.astype(jnp.int32), axis=1) - 1
    rotation = jax.random.randint(subkeys[5], (groups,), 0, per_group)
    reader = (rank_table + rotation[:, None]) % per_group
    column = 1 + rank_table // per_group
    reader_slot = jnp.where(live_flat, dest_group * per_group + reader, view_total)
    slot_table = jnp.broadcast_to(jnp.arange(view_total, dtype=jnp.int32)[:, None], (view_total, NB))
    slot_table = slot_table.at[reader_slot.reshape(-1), jnp.clip(column, 0, NB - 1).reshape(-1)].set(source_slot.reshape(-1).astype(jnp.int32), mode='drop')
    slot_scores = jax.random.randint(subkeys[6], (view_total,), 0, 1 << 20) * view_total + jnp.arange(view_total)
    view_of_slot = jnp.argsort(slot_scores, stable=True).astype(jnp.int32)
    view_slot = jnp.argsort(view_of_slot, stable=True).astype(jnp.int32)
    neighbors = view_of_slot[slot_table[view_slot]].astype(jnp.int32)
    return (view_slot, neighbors)


def draw_neighbors(key, part):
    shared = adjacency_tables(key)
    return shared[1]


def draw_view_slot(key, part):
    shared = adjacency_tables(key)
    return shared[0]


def draw_query_tokens(key, part):
    key = jax.random.fold_in(key, 5)
    drawn = jnp.clip(jax.random.normal(key, (TOKENS, HEADS * HD), jnp.float32), -5.0, 5.0)
    return drawn.astype(jnp.bfloat16)


def draw_key_tokens(key, part):
    key = jax.random.fold_in(key, 9)
    drawn = jnp.clip(jax.random.normal(key, (TOKENS, HEADS * HD), jnp.float32), -5.0, 5.0)
    return drawn.astype(jnp.bfloat16)


def level_of(stream_key, dims, cuts, smallest, top_value):
    level, own = 1.0, jax.random.fold_in(stream_key, 6)
    for dim, shards_of in cuts:
        steps = jnp.exp(jax.random.uniform(jax.random.fold_in(own, dim), (shards_of,), jnp.float32, smallest / len(cuts), top_value / len(cuts)))
        level = level * jnp.repeat(steps, dims[dim] // shards_of).reshape([-1 if axis == dim else 1 for axis in range(len(dims))])
    return level


def centred(own_key, dims, scale, reach, cuts=(), kind=jnp.bfloat16):
    factor_of = level_of(own_key, dims, cuts, -0.22, 0.18) if cuts else 1.0
    values = jax.random.normal(own_key, dims, jnp.float32) * scale * factor_of
    return jnp.minimum(jnp.maximum(values, -reach), reach).astype(kind)


def setup_inputs(seed: int = 0) -> dict:
    key_of = jax.random.split(jax.random.key(seed), 7)
    return {
        "query_tokens": draw_query_tokens(jax.random.fold_in(key_of[6], 71), 0),
        "key_tokens": draw_key_tokens(jax.random.fold_in(key_of[6], 71), 0),
        "value_tokens": centred(key_of[2], (TOKENS, HEADS * HD), 1.0, 6.0, ((0, 256),)),
        "cotangent": centred(key_of[3], (TOKENS, HEADS * HD), 1.0, 6.0, ((0, 256),)),
        "neighbors": draw_neighbors(jax.random.fold_in(key_of[6], 71), 0),
        "view_slot": draw_view_slot(jax.random.fold_in(key_of[6], 71), 0),
    }


def slot_table(neighbors, view_slot):
    slot_range = jnp.arange(VIEWS, dtype=jnp.int32)
    owner_match = view_slot[None, :] == slot_range[:, None]
    view_of_slot = lax.optimization_barrier(jnp.sum(jnp.where(owner_match, slot_range[None, :], 0), axis=1)).astype(jnp.int32)
    return view_slot[neighbors[view_of_slot]].astype(jnp.int32)

def reference(query_tokens, key_tokens, value_tokens, cotangent, neighbors, view_slot):
    score_scale = 1.0 / math.sqrt(HD)
    slot_lists = slot_table(neighbors, view_slot)
    list_width = slot_lists.shape[1]

    def split_heads(array):
        return array.reshape(VIEWS, L, HEADS, HD).transpose(2, 0, 1, 3)
    stacked = (split_heads(query_tokens), split_heads(key_tokens), split_heads(value_tokens), split_heads(cotangent))

    def one_head(arrays):
        query_all, key_all, value_all, grad_all = arrays

        def one_view(slot):
            slot_row = slot_lists[slot]
            allowed = (jnp.arange(list_width, dtype=jnp.int32) == 0) | (slot_row != slot)
            query_rows = query_all[slot].astype(jnp.float32)
            key_block = key_all[slot_row].astype(jnp.float32)
            value_block = value_all[slot_row].astype(jnp.float32)
            grad_rows = grad_all[slot].astype(jnp.float32)
            scores = jnp.einsum('qd,nkd->qnk', query_rows, key_block) * score_scale
            scores = jnp.where(allowed[None, :, None], scores, -jnp.inf)
            highest = lax.optimization_barrier(jnp.max(scores, axis=(1, 2), keepdims=True))
            log_total = highest + jnp.log(lax.optimization_barrier(jnp.sum(jnp.exp(scores - highest), axis=(1, 2), keepdims=True)))
            weights = jnp.exp(scores - log_total)
            weights_bf = lax.optimization_barrier(weights.astype(jnp.bfloat16)).astype(jnp.float32)
            out_block = jnp.einsum('qnk,nkd->qd', weights_bf, value_block).astype(jnp.bfloat16)
            row_delta = lax.optimization_barrier(jnp.sum(grad_rows * out_block.astype(jnp.float32), axis=1))
            weight_grad = jnp.einsum('qd,nkd->qnk', grad_rows, value_block)
            dscore = lax.optimization_barrier((weights * (weight_grad - row_delta[:, None, None])).astype(jnp.bfloat16)).astype(jnp.float32)
            query_part = (jnp.einsum('qnk,nkd->qd', dscore, key_block) * score_scale).astype(jnp.bfloat16)
            key_part = jnp.einsum('qnk,qd->nkd', dscore, query_rows) * score_scale
            value_part = jnp.einsum('qnk,qd->nkd', weights_bf, grad_rows)
            return (out_block, query_part, key_part, value_part)

        def one_group(totals, group):
            group_slots = group * V_G + jnp.arange(V_G, dtype=jnp.int32)
            out_block, query_part, key_part, value_part = lax.map(one_view, group_slots)
            targets = slot_lists[group_slots].reshape(-1)
            empty_grid = jnp.zeros((VIEWS, L, HD), jnp.float32)
            key_sum = empty_grid.at[targets].add(key_part.reshape(-1, L, HD))
            value_sum = empty_grid.at[targets].add(value_part.reshape(-1, L, HD))
            key_sum = lax.optimization_barrier(key_sum.astype(jnp.bfloat16)).astype(jnp.float32)
            value_sum = lax.optimization_barrier(value_sum.astype(jnp.bfloat16)).astype(jnp.float32)
            return ((totals[0] + key_sum, totals[1] + value_sum), (out_block, query_part))
        start_grid = jnp.zeros((VIEWS, L, HD), jnp.float32)
        totals, (out_all, query_all_grad) = lax.scan(one_group, (start_grid, start_grid), jnp.arange(N_VIEW, dtype=jnp.int32))
        return (out_all.reshape(VIEWS, L, HD), query_all_grad.reshape(VIEWS, L, HD), totals[0].astype(jnp.bfloat16), totals[1].astype(jnp.bfloat16))
    results = lax.map(one_head, stacked)

    def merge_heads(array):
        return array.transpose(1, 2, 0, 3).reshape(TOKENS, HEADS * HD)
    return (merge_heads(results[0]), merge_heads(results[1]), merge_heads(results[2]), merge_heads(results[3]))
```

```python
import functools
import math

import jax
import jax.numpy as jnp
from jax import lax
from jax.experimental import pallas as pl
from jax.experimental.pallas import tpu as pltpu
from jax.sharding import PartitionSpec as P

MESH = pl.DeviceIdType.MESH
GROUPS = 8
HEADS = 32
PER_GROUP = 8
RANKS = 4
ROWS = 128
HD = 128
LENGTH = 512
OTHERS = GROUPS - 1
SCALE = 1.0 / math.sqrt(HD)
EXP2_SCALE = math.log2(math.e) / math.sqrt(HD)
BF = jnp.bfloat16
F32 = jnp.float32


def dot_nt(a, b):
    return lax.dot_general(a, b, (((1,), (1,)), ((), ())), preferred_element_type=F32)


def dot_nn(a, b):
    return lax.dot_general(a, b, (((1,), (0,)), ((), ())), preferred_element_type=F32)


def kernel(
    neighbors, view_slot, q_in, k_in, v_in, g_in,
    o_out, dq_out, dk_out, dv_out,
    qh, kh, vh, gh,
    send_k, send_v, far_k, far_v,
    oh, dqh, dkh, dvh,
    acc_k, acc_v, ret_k, ret_v, back_k, back_v,
    table,
    in_send, in_recv, z_send, z_recv, ret_send, ret_recv_k, ret_recv_v, out_send, out_recv,
):
    group = lax.axis_index("view")
    head = lax.axis_index("head")
    row_y, col_x, core = head // 8, (head // 2) % 4, head % 2

    def plane_peer(step):
        dy, dx, dc = step // 8, (step // 2) % 4, step % 2
        return (((row_y + dy) % 4) * 4 + (col_x + dx) % 4) * 2 + (core + dc) % 2

    def for_peers(body):
        def run(step, carry):
            body(plane_peer(step))
            return carry

        lax.fori_loop(1, HEADS, run, 0)

    def columns(index):
        return pl.ds(pl.multiple_of(index * HD, HD), HD)

    barrier = pltpu.get_barrier_semaphore()

    def greet(peer):
        pl.semaphore_signal(barrier, inc=1, device_id=(group, peer), device_id_type=MESH)

    for_peers(greet)
    for step in range(1, GROUPS):
        pl.semaphore_signal(
            barrier, inc=1, device_id=((group + step) % GROUPS, head), device_id_type=MESH
        )
    pl.semaphore_wait(barrier, HEADS - 1 + OTHERS)

    def scatter_heads(index, source, target):
        def send(peer):
            pltpu.make_async_remote_copy(
                src_ref=source.at[:, columns(peer)],
                dst_ref=target.at[head],
                send_sem=in_send.at[index],
                recv_sem=in_recv.at[index],
                device_id=(group, peer),
                device_id_type=MESH,
            ).start()

        for_peers(send)
        pltpu.make_async_copy(
            source.at[:, columns(head)], target.at[head], in_recv.at[index]
        ).start()

    def wait_heads(index, target):
        pltpu.make_async_copy(target, target, in_recv.at[index]).wait()

    scatter_heads(0, k_in, kh)
    scatter_heads(1, v_in, vh)

    def read_links(view, carry):
        slots, wanted = carry
        slot = view_slot[view]
        other = view_slot[neighbors[view, 1]]
        slot_group, slot_place = slot >> 3, slot & 7
        other_group, other_place = other >> 3, other & 7
        source = (other_group - group + 7) & 7
        reader = (slot_group - group + 7) & 7
        own = slot_group == group
        read = (other_group == group) & (reader != 7)
        slots = tuple(
            jnp.where(own & (slot_place == place), source, slots[place])
            for place in range(PER_GROUP)
        )
        wanted = tuple(
            jnp.where(read & (reader == index), other_place, wanted[index])
            for index in range(OTHERS)
        )
        return slots, wanted

    slots, wanted = lax.fori_loop(
        0,
        PER_GROUP * GROUPS,
        read_links,
        ((jnp.int32(7),) * PER_GROUP, (jnp.int32(-1),) * OTHERS),
    )
    for place in range(PER_GROUP):
        table[0, place] = jnp.where(slots[place] == 7, 0, slots[place])
        table[1, place] = jnp.where(slots[place] == 7, 1, 0)
        before = jnp.int32(-1)
        for earlier in range(place):
            before = jnp.where(
                (slots[earlier] == slots[place]) & (slots[place] != 7), earlier, before
            )
        table[2, place] = before

    def exchange(index, source, stage, target):
        for reader in (3, 2, 4, 1, 5, 0, 6):
            place = jnp.maximum(wanted[reader], 0)
            stage[reader] = source[pl.ds(place * RANKS, RANKS)]
            pltpu.make_async_remote_copy(
                src_ref=stage.at[reader],
                dst_ref=target.at[OTHERS - 1 - reader],
                send_sem=z_send.at[index],
                recv_sem=z_recv.at[index],
                device_id=((group + 1 + reader) % GROUPS, head),
                device_id_type=MESH,
            ).start()

    wait_heads(0, kh)
    exchange(0, kh, send_k, far_k)
    scatter_heads(2, q_in, qh)
    wait_heads(1, vh)
    exchange(1, vh, send_v, far_v)
    scatter_heads(3, g_in, gh)
    wait_heads(2, qh)
    wait_heads(3, gh)
    for index, target in ((0, far_k), (1, far_v)):
        pltpu.make_async_copy(target, target, z_recv.at[index]).wait()

    def attend(place, carry):
        source = table[0, place]
        off = table[1, place].astype(F32) * 1e30
        before = table[2, place]
        rows = pl.ds(place * RANKS, RANKS)
        k, v = kh[rows].reshape(LENGTH, HD), vh[rows].reshape(LENGTH, HD)
        q, g = qh[rows].reshape(LENGTH, HD), gh[rows].reshape(LENGTH, HD)
        rk, rv = far_k[source].reshape(LENGTH, HD), far_v[source].reshape(LENGTH, HD)
        s_own, s_far = dot_nt(k, q), dot_nt(rk, q)
        highest = EXP2_SCALE * jnp.maximum(
            jnp.max(s_own, 0, keepdims=True), jnp.max(s_far, 0, keepdims=True) - off
        )
        e_own = jnp.exp2(s_own * EXP2_SCALE - highest)
        e_far = jnp.exp2(s_far * EXP2_SCALE - (highest + off))
        inverse = 1.0 / (jnp.sum(e_own, 0, keepdims=True) + jnp.sum(e_far, 0, keepdims=True))
        w_own, w_far = e_own * inverse, e_far * inverse
        b_own, b_far = w_own.astype(BF), w_far.astype(BF)
        out = (dot_nn(v.T, b_own) + dot_nn(rv.T, b_far)).astype(BF)
        oh[rows] = out.T.reshape(RANKS, ROWS, HD)
        delta = jnp.sum(g.T.astype(F32) * out.astype(F32), 0, keepdims=True)
        d_own = (w_own * (dot_nt(v, g) - delta)).astype(BF)
        d_far = (w_far * (dot_nt(rv, g) - delta)).astype(BF)
        grad = ((dot_nn(k.T, d_own) + dot_nn(rk.T, d_far)) * SCALE).astype(BF)
        dqh[rows] = grad.T.reshape(RANKS, ROWS, HD)
        dkh[rows] = (dot_nn(d_own, q) * SCALE).astype(BF).reshape(RANKS, ROWS, HD)
        dvh[rows] = dot_nn(b_own, g).astype(BF).reshape(RANKS, ROWS, HD)
        chained = jnp.maximum(before, 0)
        old_k, old_v = acc_k[chained], acc_v[chained]
        acc_k[place] = dot_nn(d_far, q) * SCALE + jnp.where(before >= 0, old_k, 0.0)
        acc_v[place] = dot_nn(b_far, g) + jnp.where(before >= 0, old_v, 0.0)
        return carry

    lax.fori_loop(0, PER_GROUP, attend, 0)

    returns = ((acc_k, ret_k, back_k, ret_recv_k), (acc_v, ret_v, back_v, ret_recv_v))
    last = []
    for source in range(OTHERS):
        final = jnp.int32(0)
        for place in range(PER_GROUP):
            final = jnp.where(slots[place] == source, place, final)
        last.append(final)
    for index, (acc, ret, back, recv) in enumerate(returns):
        for source in (3, 2, 4, 1, 5, 0, 6):
            ret[source] = acc[last[source]].astype(BF).reshape(RANKS, ROWS, HD)
    for rank in range(RANKS):
        for index, (acc, ret, back, recv) in enumerate(returns):
            for source in (3, 2, 4, 1, 5, 0, 6):
                pltpu.make_async_remote_copy(
                    src_ref=ret.at[source, rank],
                    dst_ref=back.at[rank, OTHERS - 1 - source],
                    send_sem=ret_send.at[index],
                    recv_sem=recv.at[rank],
                    device_id=((group + 1 + source) % GROUPS, head),
                    device_id_type=MESH,
                ).start()

    def gather_block(index, block, source, target):
        pltpu.make_async_remote_copy(
            src_ref=source.at[block],
            dst_ref=target.at[:, columns(head)],
            send_sem=out_send.at[index],
            recv_sem=out_recv.at[index],
            device_id=(group, block),
            device_id_type=MESH,
        ).start()

    def gather_own(index, source, target):
        pltpu.make_async_copy(
            source.at[head], target.at[:, columns(head)], out_recv.at[index]
        ).start()

    for_peers(lambda peer: gather_block(0, peer, oh, o_out))
    gather_own(0, oh, o_out)
    for_peers(lambda peer: gather_block(1, peer, dqh, dq_out))
    gather_own(1, dqh, dq_out)

    first, second = jnp.int32(8), jnp.int32(-1)
    for reader in range(OTHERS):
        first = jnp.where(
            (wanted[reader] >= 0) & (wanted[reader] < first), wanted[reader], first
        )
        second = jnp.maximum(second, wanted[reader])

    for rank in range(RANKS):
        for index, (acc, ret, back, recv) in enumerate(returns):
            target = (dkh, dvh)[index]
            output = (dk_out, dv_out)[index]
            pltpu.make_async_copy(back.at[rank], back.at[rank], recv.at[rank]).wait()
            first_sum = jnp.zeros((ROWS, HD), F32)
            second_sum = jnp.zeros((ROWS, HD), F32)
            for reader in range(OTHERS):
                part = back[rank, reader].astype(F32)
                first_sum += jnp.where(wanted[reader] == first, part, 0.0)
                second_sum += jnp.where(wanted[reader] == second, part, 0.0)
            for place in range(PER_GROUP):
                block = place * RANKS + rank
                extra = jnp.where(
                    place == first, first_sum, jnp.where(place == second, second_sum, 0.0)
                )
                target[block] = (target[block].astype(F32) + extra).astype(BF)

                @pl.when(block != head)
                def _():
                    gather_block(2 + index, block, target, output)

                @pl.when(block == head)
                def _():
                    gather_own(2 + index, target, output)

    for index, output in enumerate((o_out, dq_out, dk_out, dv_out)):
        pltpu.make_async_copy(output, output, out_recv.at[index]).wait()
    for index, source in enumerate((kh, vh, qh, gh)):
        blocks = source.at[pl.ds(0, HEADS - 1)]
        pltpu.make_async_copy(blocks, blocks, in_send.at[index]).wait()
        pltpu.make_async_copy(blocks, blocks, out_send.at[index]).wait()
    for index, stage in ((0, send_k), (1, send_v)):
        pltpu.make_async_copy(stage, stage, z_send.at[index]).wait()
    for index, stage in ((0, ret_k), (1, ret_v)):
        pltpu.make_async_copy(stage, stage, ret_send.at[index]).wait()


def on_device(query_tokens, key_tokens, value_tokens, cotangent, neighbors, view_slot):
    heads_buffer = pltpu.VMEM((HEADS, ROWS, HD), BF)
    far_buffer = pltpu.VMEM((OTHERS, RANKS, ROWS, HD), BF)
    back_buffer = pltpu.VMEM((RANKS, OTHERS, ROWS, HD), BF)
    sum_buffer = pltpu.VMEM((PER_GROUP, LENGTH, HD), F32)
    dma = pltpu.SemaphoreType.DMA
    smem = pl.BlockSpec(memory_space=pltpu.SMEM)
    anywhere = pl.BlockSpec(memory_space=pl.ANY)
    out = jax.ShapeDtypeStruct(query_tokens.shape, BF)
    return pl.pallas_call(
        kernel,
        out_shape=(out,) * 4,
        in_specs=[smem] * 2 + [anywhere] * 4,
        out_specs=(anywhere,) * 4,
        scratch_shapes=[heads_buffer] * 4
        + [far_buffer] * 4
        + [heads_buffer] * 4
        + [sum_buffer] * 2
        + [far_buffer] * 2
        + [back_buffer] * 2
        + [pltpu.SMEM((3, PER_GROUP), jnp.int32)]
        + [dma((4,))] * 2
        + [dma((2,))] * 3
        + [dma((RANKS,))] * 2
        + [dma((4,))] * 2,
        compiler_params=pltpu.CompilerParams(
            collective_id=0, has_side_effects=True, vmem_limit_bytes=56 << 20
        ),
    )(neighbors, view_slot, query_tokens, key_tokens, value_tokens, cotangent)


def solution(mesh):
    rows = P(("view", "head"), None)
    return jax.shard_map(
        on_device,
        mesh=mesh,
        in_specs=(rows, rows, rows, rows, P(), P()),
        out_specs=(rows, rows, rows, rows),
        check_vma=False,
    )
```

```python
import functools
import math

import jax
import jax.numpy as jnp
from jax import lax
from jax.experimental import pallas as pl
from jax.experimental.pallas import tpu as pltpu
from jax.sharding import PartitionSpec as P

MESH = pl.DeviceIdType.MESH
GROUPS = 8
HEADS = 32
PER_GROUP = 8
RANKS = 4
ROWS = 128
HD = 128
LENGTH = 512
OTHERS = GROUPS - 1
SCALE = 1.0 / math.sqrt(HD)
EXP2_SCALE = math.log2(math.e) / math.sqrt(HD)
BF = jnp.bfloat16
F32 = jnp.float32


def ring_distance(step):
    return min(step, 4 - step)


PEERS = sorted(
    (
        (dy, dx, dc)
        for dy in range(4)
        for dx in range(4)
        for dc in range(2)
        if (dy, dx, dc) != (0, 0, 0)
    ),
    key=lambda step: (-ring_distance(step[0]) - ring_distance(step[1]), step),
)

POOL_K = {7: (0, 2), 6: (2, 2), 5: (4, 2), 4: (6, 1), 1: (7, 2), 2: (9, 2), 3: (11, 1)}
POOL_V = {7: (0, 2), 6: (2, 2), 5: (4, 1), 1: (5, 2), 2: (7, 2), 3: (9, 2), 4: (11, 1)}
POOL = 12
CHOICES = ((5, 1), (2, 7), (6, 1), (3, 7))


def dot_nt(a, b):
    return lax.dot_general(a, b, (((1,), (1,)), ((), ())), preferred_element_type=F32)


def dot_nn(a, b):
    return lax.dot_general(a, b, (((1,), (0,)), ((), ())), preferred_element_type=F32)


def kernel(
    neighbors, view_slot, q_in, k_in, v_in, g_in,
    o_out, dq_out, dk_out, dv_out,
    qh, kh, vh, gh,
    stage_k, stage_v, chosen, pool_k, pool_v,
    oh, dqh, dkh, dvh,
    exp_own, out_own, stats, d_far_all,
    acc_k, acc_v, ret_k, ret_v, back_k, back_v,
    table,
    in_send, in_recv, z_send, z_recv_k, z_recv_v,
    ret_send, ret_recv_k, ret_recv_v, out_send, out_recv,
):
    group = lax.axis_index("view")
    head = lax.axis_index("head")
    row_y, col_x, core = head // 8, (head // 2) % 4, head % 2

    def for_peers(body):
        for dy, dx, dc in PEERS:
            body((((row_y + dy) % 4) * 4 + (col_x + dx) % 4) * 2 + (core + dc) % 2)

    def columns(index):
        return pl.ds(pl.multiple_of(index * HD, HD), HD)

    barrier = pltpu.get_barrier_semaphore()

    def greet(peer):
        pl.semaphore_signal(barrier, inc=1, device_id=(group, peer), device_id_type=MESH)

    for_peers(greet)
    for step in range(1, GROUPS):
        pl.semaphore_signal(
            barrier, inc=1, device_id=((group + step) % GROUPS, head), device_id_type=MESH
        )
    pl.semaphore_wait(barrier, HEADS - 1 + OTHERS)

    def scatter_heads(index, source, target):
        def send(peer):
            pltpu.make_async_remote_copy(
                src_ref=source.at[:, columns(peer)],
                dst_ref=target.at[head],
                send_sem=in_send.at[index],
                recv_sem=in_recv.at[index],
                device_id=(group, peer),
                device_id_type=MESH,
            ).start()

        for_peers(send)
        pltpu.make_async_copy(
            source.at[:, columns(head)], target.at[head], in_recv.at[index]
        ).start()

    def wait_heads(index, target):
        pltpu.make_async_copy(target, target, in_recv.at[index]).wait()

    scatter_heads(0, k_in, kh)
    scatter_heads(1, v_in, vh)

    def read_links(view, carry):
        named, lowest, highest, chosen_place, wanted = carry
        slot = view_slot[view]
        other = view_slot[neighbors[1, view]]
        slot_group, slot_place = slot >> 3, slot & 7
        other_group, other_place = other >> 3, other & 7
        own = slot_group == group
        far = slot_group != other_group
        reader = (slot_group - group) & 7
        owner = (other_group - group) & 7
        named = tuple(
            jnp.where(own & (slot_place == place), other, named[place])
            for place in range(PER_GROUP)
        )
        lowest = tuple(
            jnp.where(far & (owner == index), jnp.minimum(other_place, lowest[index]), lowest[index])
            for index in range(GROUPS)
        )
        highest = jnp.where(far & (owner == 0), jnp.maximum(other_place, highest), highest)
        chosen_place = tuple(
            jnp.where((owner == first) & (reader == second), other_place, current)
            for (first, second), current in zip(CHOICES, chosen_place)
        )
        wanted = tuple(
            jnp.where((owner == 0) & (reader == index), other_place, wanted[index])
            for index in range(GROUPS)
        )
        return named, lowest, highest, chosen_place, wanted

    zero = jnp.int32(0)
    named, lowest, highest, chosen_place, wanted = lax.fori_loop(
        0,
        PER_GROUP * GROUPS,
        read_links,
        (
            (zero,) * PER_GROUP,
            (zero + 7,) * GROUPS,
            zero,
            (zero,) * len(CHOICES),
            (zero - 1,) * GROUPS,
        ),
    )
    exports = (lowest[0], highest)
    chosen_second = tuple(
        place > lowest[owner] for (owner, _), place in zip(CHOICES, chosen_place)
    )
    offsets = tuple(((slot >> 3) - group) & 7 for slot in named)
    for place in range(PER_GROUP):
        index_k, index_v = zero, zero
        for offset in range(1, GROUPS):
            second = jnp.where((named[place] & 7) > lowest[offset], 1, 0)
            here = offsets[place] == offset
            start, views = POOL_K[offset]
            index_k = jnp.where(here, start + (second if views == 2 else 0), index_k)
            start, views = POOL_V[offset]
            index_v = jnp.where(here, start + (second if views == 2 else 0), index_v)
        before = zero - 1
        for earlier in range(place):
            before = jnp.where(
                (offsets[earlier] == offsets[place]) & (offsets[place] != 0), earlier, before
            )
        table[0, place] = index_k
        table[1, place] = index_v
        table[2, place] = jnp.where(offsets[place] == 0, 1, 0)
        table[3, place] = before

    def along_z(source, target, sends, receives, step):
        pltpu.make_async_remote_copy(
            src_ref=source,
            dst_ref=target,
            send_sem=sends,
            recv_sem=receives,
            device_id=((group + step) % GROUPS, head),
            device_id_type=MESH,
        ).start()

    pools = ((kh, stage_k, pool_k, z_recv_k, POOL_K), (vh, stage_v, pool_v, z_recv_v, POOL_V))

    def landing(array, offset):
        start, views = pools[array][4][offset]
        return pools[array][2].at[pl.ds(start, views)]

    def wait_landing(array, offset):
        here = landing(array, offset)
        pltpu.make_async_copy(here, here, pools[array][3].at[offset - 1]).wait()

    def first_hop(array):
        source, stage, _, receives, _ = pools[array]
        for index in range(2):
            stage[index] = source[pl.ds(exports[index] * RANKS, RANKS)]
        along_z(stage, landing(array, 7), z_send.at[array, 0], receives.at[6], 1)
        along_z(stage, landing(array, 1), z_send.at[array, 1], receives.at[0], 7)

    def forward(array, offset):
        step = 1 if offset > 3 else 7
        target = offset - 1 if step == 1 else offset + 1
        wait_landing(array, offset)
        along_z(
            landing(array, offset),
            landing(array, target),
            z_send.at[array, 1 + offset],
            pools[array][3].at[target - 1],
            step,
        )

    def forward_chosen(array, offset, index):
        step = 1 if offset > 3 else 7
        target = offset - 1 if step == 1 else offset + 1
        wait_landing(array, offset)
        start = pools[array][4][offset][0]
        pool = pools[array][2]
        chosen[index] = jnp.where(chosen_second[index], pool[start + 1], pool[start])
        along_z(
            chosen.at[pl.ds(index, 1)],
            landing(array, target),
            z_send.at[array, 1 + offset],
            pools[array][3].at[target - 1],
            step,
        )

    def heads_of(ref, place):
        return ref[pl.ds(place * RANKS, RANKS)].reshape(LENGTH, HD)

    def own_forward(place, carry):
        k, v, q = heads_of(kh, place), heads_of(vh, place), heads_of(qh, place)
        scores = dot_nt(k, q)
        top = EXP2_SCALE * jnp.max(scores, 0, keepdims=True)
        exps = jnp.exp2(scores * EXP2_SCALE - top)
        exp_own[place] = exps
        out_own[place] = dot_nn(v.T, exps.astype(BF))
        stats[place, 0:1] = top
        stats[place, 1:2] = jnp.sum(exps, 0, keepdims=True)
        return carry

    def far_part(place, carry):
        index_k, index_v = table[0, place], table[1, place]
        off = table[2, place].astype(F32) * 1e30
        before = table[3, place]
        rows = pl.ds(place * RANKS, RANKS)
        q, g = heads_of(qh, place), heads_of(gh, place)
        k, v = pool_k[index_k].reshape(LENGTH, HD), pool_v[index_v].reshape(LENGTH, HD)
        scores = dot_nt(k, q)
        own_top = stats[place, 0:1]
        top = jnp.maximum(own_top, EXP2_SCALE * jnp.max(scores, 0, keepdims=True) - off)
        exps = jnp.exp2(scores * EXP2_SCALE - (top + off))
        rescale = jnp.exp2(own_top - top)
        inverse = 1.0 / (stats[place, 1:2] * rescale + jnp.sum(exps, 0, keepdims=True))
        own_factor = rescale * inverse
        weights = exps * inverse
        weights_bf = weights.astype(BF)
        out = (out_own[place] * own_factor + dot_nn(v.T, weights_bf)).astype(BF)
        oh[rows] = out.T.reshape(RANKS, ROWS, HD)
        delta = jnp.sum(g.T.astype(F32) * out.astype(F32), 0, keepdims=True)
        dscore = (weights * (dot_nt(v, g) - delta)).astype(BF)
        d_far_all[place] = dscore
        stats[place, 2:3] = own_factor
        stats[place, 3:4] = delta
        chained = jnp.maximum(before, 0)
        old_k, old_v = acc_k[chained], acc_v[chained]
        acc_k[place] = dot_nn(dscore, q) * SCALE + jnp.where(before >= 0, old_k, 0.0)
        acc_v[place] = dot_nn(weights_bf, g) + jnp.where(before >= 0, old_v, 0.0)
        return carry

    def own_backward(place, carry):
        rows = pl.ds(place * RANKS, RANKS)
        k, v = heads_of(kh, place), heads_of(vh, place)
        q, g = heads_of(qh, place), heads_of(gh, place)
        far_k = pool_k[table[0, place]].reshape(LENGTH, HD)
        weights = exp_own[place] * stats[place, 2:3]
        dvh[rows] = dot_nn(weights.astype(BF), g).astype(BF).reshape(RANKS, ROWS, HD)
        dscore = (weights * (dot_nt(v, g) - stats[place, 3:4])).astype(BF)
        dkh[rows] = (dot_nn(dscore, q) * SCALE).astype(BF).reshape(RANKS, ROWS, HD)
        grad = (dot_nn(k.T, dscore) + dot_nn(far_k.T, d_far_all[place])) * SCALE
        dqh[rows] = grad.astype(BF).T.reshape(RANKS, ROWS, HD)
        return carry

    wait_heads(0, kh)
    first_hop(0)
    scatter_heads(2, q_in, qh)
    forward(0, 7)
    forward(0, 1)
    wait_heads(1, vh)
    first_hop(1)
    scatter_heads(3, g_in, gh)
    forward(0, 6)
    forward_chosen(0, 2, 1)
    forward(1, 7)
    forward(1, 1)
    forward_chosen(0, 5, 0)
    wait_heads(2, qh)
    lax.fori_loop(0, 2, own_forward, 0)
    forward_chosen(1, 6, 2)
    forward(1, 2)
    lax.fori_loop(2, 5, own_forward, 0)
    forward_chosen(1, 3, 3)
    lax.fori_loop(5, PER_GROUP, own_forward, 0)
    wait_heads(3, gh)
    wait_landing(0, 4)
    wait_landing(0, 3)
    wait_landing(1, 5)
    wait_landing(1, 4)
    lax.fori_loop(0, PER_GROUP, far_part, 0)

    returns = ((acc_k, ret_k, back_k, ret_recv_k), (acc_v, ret_v, back_v, ret_recv_v))
    order = (4, 3, 5, 2, 6, 1, 7)
    last = {}
    for offset in order:
        final = zero
        for place in range(PER_GROUP):
            final = jnp.where(offsets[place] == offset, place, final)
        last[offset] = final
    for rank in range(RANKS):
        for index, (acc, ret, back, recv) in enumerate(returns):
            for offset in order:
                ret[offset - 1, rank] = acc[last[offset], pl.ds(rank * ROWS, ROWS)].astype(BF)
                along_z(
                    ret.at[offset - 1, rank],
                    back.at[rank, OTHERS - offset],
                    ret_send.at[index],
                    recv.at[rank],
                    offset,
                )

    def gather_block(index, block, source, target):
        pltpu.make_async_remote_copy(
            src_ref=source.at[block],
            dst_ref=target.at[:, columns(head)],
            send_sem=out_send.at[index],
            recv_sem=out_recv.at[index],
            device_id=(group, block),
            device_id_type=MESH,
        ).start()

    def gather_own(index, source, target):
        pltpu.make_async_copy(
            source.at[head], target.at[:, columns(head)], out_recv.at[index]
        ).start()

    for_peers(lambda peer: gather_block(0, peer, oh, o_out))
    gather_own(0, oh, o_out)
    lax.fori_loop(0, PER_GROUP, own_backward, 0)
    for_peers(lambda peer: gather_block(1, peer, dqh, dq_out))
    gather_own(1, dqh, dq_out)

    for rank in range(RANKS):
        for index, (acc, ret, back, recv) in enumerate(returns):
            target = (dkh, dvh)[index]
            output = (dk_out, dv_out)[index]
            pltpu.make_async_copy(back.at[rank], back.at[rank], recv.at[rank]).wait()
            first_sum = jnp.zeros((ROWS, HD), F32)
            second_sum = jnp.zeros((ROWS, HD), F32)
            for offset in range(1, GROUPS):
                part = back[rank, offset - 1].astype(F32)
                first_sum += jnp.where(wanted[offset] == exports[0], part, 0.0)
                second_sum += jnp.where(wanted[offset] == exports[1], part, 0.0)
            for place in range(PER_GROUP):
                block = place * RANKS + rank
                extra = jnp.where(
                    place == exports[0],
                    first_sum,
                    jnp.where(place == exports[1], second_sum, 0.0),
                )
                target[block] = (target[block].astype(F32) + extra).astype(BF)

                @pl.when(block != head)
                def _():
                    gather_block(2 + index, block, target, output)

                @pl.when(block == head)
                def _():
                    gather_own(2 + index, target, output)

    for index, output in enumerate((o_out, dq_out, dk_out, dv_out)):
        pltpu.make_async_copy(output, output, out_recv.at[index]).wait()
    for index, source in enumerate((kh, vh, qh, gh)):
        blocks = source.at[pl.ds(0, HEADS - 1)]
        pltpu.make_async_copy(blocks, blocks, in_send.at[index]).wait()
        pltpu.make_async_copy(blocks, blocks, out_send.at[index]).wait()
    for array, stage in ((0, stage_k), (1, stage_v)):
        one = stage.at[pl.ds(0, 1)]
        pltpu.make_async_copy(stage, stage, z_send.at[array, 0]).wait()
        pltpu.make_async_copy(stage, stage, z_send.at[array, 1]).wait()
        for offset in ((7, 1, 6, 2, 5), (7, 1, 6, 2, 3))[array]:
            single = (array, offset) in ((0, 5), (0, 2), (1, 6), (1, 3))
            sent = one if single else stage
            pltpu.make_async_copy(sent, sent, z_send.at[array, 1 + offset]).wait()
    for index, ret in ((0, ret_k), (1, ret_v)):
        pltpu.make_async_copy(ret, ret, ret_send.at[index]).wait()


def on_device(query_tokens, key_tokens, value_tokens, cotangent, neighbors, view_slot):
    heads_buffer = pltpu.VMEM((HEADS, ROWS, HD), BF)

    def views(count):
        return pltpu.VMEM((count, RANKS, ROWS, HD), BF)

    back_buffer = pltpu.VMEM((RANKS, OTHERS, ROWS, HD), BF)
    sum_buffer = pltpu.VMEM((PER_GROUP, LENGTH, HD), F32)
    dma = pltpu.SemaphoreType.DMA
    smem = pl.BlockSpec(memory_space=pltpu.SMEM)
    anywhere = pl.BlockSpec(memory_space=pl.ANY)
    out = jax.ShapeDtypeStruct(query_tokens.shape, BF)
    return pl.pallas_call(
        kernel,
        out_shape=(out,) * 4,
        in_specs=[smem] * 2 + [anywhere] * 4,
        out_specs=(anywhere,) * 4,
        scratch_shapes=[heads_buffer] * 4
        + [views(2)] * 2
        + [views(len(CHOICES))]
        + [views(POOL)] * 2
        + [heads_buffer] * 4
        + [
            pltpu.VMEM((PER_GROUP, LENGTH, LENGTH), F32),
            pltpu.VMEM((PER_GROUP, HD, LENGTH), F32),
            pltpu.VMEM((PER_GROUP, 8, LENGTH), F32),
            pltpu.VMEM((PER_GROUP, LENGTH, LENGTH), BF),
        ]
        + [sum_buffer] * 2
        + [views(OTHERS)] * 2
        + [back_buffer] * 2
        + [pltpu.SMEM((4, PER_GROUP), jnp.int32)]
        + [dma((4,))] * 2
        + [dma((2, 9))]
        + [dma((OTHERS,))] * 2
        + [dma((2,))]
        + [dma((RANKS,))] * 2
        + [dma((4,))] * 2,
        compiler_params=pltpu.CompilerParams(
            collective_id=0, has_side_effects=True, vmem_limit_bytes=56 << 20
        ),
    )(neighbors.T, view_slot, query_tokens, key_tokens, value_tokens, cotangent)


def solution(mesh):
    rows = P(("view", "head"), None)
    return jax.shard_map(
        on_device,
        mesh=mesh,
        in_specs=(rows, rows, rows, rows, P(), P()),
        out_specs=(rows, rows, rows, rows),
        check_vma=False,
    )
```

```python
import functools
import math

import jax
import jax.numpy as jnp
from jax import lax
from jax.experimental import pallas as pl
from jax.experimental.pallas import tpu as pltpu
from jax.sharding import PartitionSpec as P

MESH = pl.DeviceIdType.MESH
GROUPS = 8
HEADS = 32
PER_GROUP = 8
RANKS = 4
ROWS = 128
HD = 128
LENGTH = 512
OTHERS = GROUPS - 1
PARTS = 4
SCALE = 1.0 / math.sqrt(HD)
EXP2_SCALE = math.log2(math.e) / math.sqrt(HD)
BF = jnp.bfloat16
F32 = jnp.float32


def ring_distance(step):
    return min(step, 4 - step)


PEERS = sorted(
    (
        (dy, dx, dc)
        for dy in range(4)
        for dx in range(4)
        for dc in range(2)
        if (dy, dx, dc) != (0, 0, 0)
    ),
    key=lambda step: (-ring_distance(step[0]) - ring_distance(step[1]), step),
)

POOL_K = {7: (0, 2), 6: (2, 2), 5: (4, 2), 4: (6, 1), 1: (7, 2), 2: (9, 2), 3: (11, 1)}
POOL_V = {7: (0, 2), 6: (2, 2), 5: (4, 1), 1: (5, 2), 2: (7, 2), 3: (9, 2), 4: (11, 1)}
POOL = 12
CHOICES = ((5, 1), (2, 7), (6, 1), (3, 7))


def dot_nt(a, b):
    return lax.dot_general(a, b, (((1,), (1,)), ((), ())), preferred_element_type=F32)


def dot_nn(a, b):
    return lax.dot_general(a, b, (((1,), (0,)), ((), ())), preferred_element_type=F32)


def kernel(
    neighbors, view_slot, q_in, k_in, v_in, g_in,
    o_out, dq_out, dk_out, dv_out,
    qh, kh, vh, gh,
    stage_k, stage_v, chosen, pool_k, pool_v,
    oh, dqh, dkh, dvh,
    exp_own, out_own, stats, weights_far, d_far_all,
    acc_k, acc_v, ret_k, ret_v, back_k, back_v,
    table,
    in_send, in_recv, z_send, z_recv_k, z_recv_v,
    ret_send, ret_recv_k, ret_recv_v, out_send, out_recv,
):
    group = lax.axis_index("view")
    head = lax.axis_index("head")
    row_y, col_x, core = head // 8, (head // 2) % 4, head % 2

    def for_peers(body):
        for dy, dx, dc in PEERS:
            body((((row_y + dy) % 4) * 4 + (col_x + dx) % 4) * 2 + (core + dc) % 2)

    def columns(index):
        return pl.ds(pl.multiple_of(index * HD, HD), HD)

    barrier = pltpu.get_barrier_semaphore()

    def greet(peer):
        pl.semaphore_signal(barrier, inc=1, device_id=(group, peer), device_id_type=MESH)

    for_peers(greet)
    for step in range(1, GROUPS):
        pl.semaphore_signal(
            barrier, inc=1, device_id=((group + step) % GROUPS, head), device_id_type=MESH
        )
    pl.semaphore_wait(barrier, HEADS - 1 + OTHERS)

    def scatter_heads(index, source, target):
        def send(peer):
            pltpu.make_async_remote_copy(
                src_ref=source.at[:, columns(peer)],
                dst_ref=target.at[head],
                send_sem=in_send.at[index],
                recv_sem=in_recv.at[index],
                device_id=(group, peer),
                device_id_type=MESH,
            ).start()

        for_peers(send)
        pltpu.make_async_copy(
            source.at[:, columns(head)], target.at[head], in_recv.at[index]
        ).start()

    def wait_heads(index, target):
        pltpu.make_async_copy(target, target, in_recv.at[index]).wait()

    scatter_heads(0, k_in, kh)
    scatter_heads(1, v_in, vh)

    def read_links(view, carry):
        named, lowest, highest, chosen_place, wanted = carry
        slot = view_slot[view]
        other = view_slot[neighbors[1, view]]
        slot_group, slot_place = slot >> 3, slot & 7
        other_group, other_place = other >> 3, other & 7
        own = slot_group == group
        far = slot_group != other_group
        reader = (slot_group - group) & 7
        owner = (other_group - group) & 7
        named = tuple(
            jnp.where(own & (slot_place == place), other, named[place])
            for place in range(PER_GROUP)
        )
        lowest = tuple(
            jnp.where(far & (owner == index), jnp.minimum(other_place, lowest[index]), lowest[index])
            for index in range(GROUPS)
        )
        highest = jnp.where(far & (owner == 0), jnp.maximum(other_place, highest), highest)
        chosen_place = tuple(
            jnp.where((owner == first) & (reader == second), other_place, current)
            for (first, second), current in zip(CHOICES, chosen_place)
        )
        wanted = tuple(
            jnp.where((owner == 0) & (reader == index), other_place, wanted[index])
            for index in range(GROUPS)
        )
        return named, lowest, highest, chosen_place, wanted

    zero = jnp.int32(0)
    named, lowest, highest, chosen_place, wanted = lax.fori_loop(
        0,
        PER_GROUP * GROUPS,
        read_links,
        (
            (zero,) * PER_GROUP,
            (zero + 7,) * GROUPS,
            zero,
            (zero,) * len(CHOICES),
            (zero - 1,) * GROUPS,
        ),
    )
    exports = (lowest[0], highest)
    chosen_second = tuple(
        place > lowest[owner] for (owner, _), place in zip(CHOICES, chosen_place)
    )
    offsets = tuple(((slot >> 3) - group) & 7 for slot in named)
    for place in range(PER_GROUP):
        index_k, index_v = zero, zero
        for offset in range(1, GROUPS):
            second = jnp.where((named[place] & 7) > lowest[offset], 1, 0)
            here = offsets[place] == offset
            start, views = POOL_K[offset]
            index_k = jnp.where(here, start + (second if views == 2 else 0), index_k)
            start, views = POOL_V[offset]
            index_v = jnp.where(here, start + (second if views == 2 else 0), index_v)
        before = zero - 1
        for earlier in range(place):
            before = jnp.where(
                (offsets[earlier] == offsets[place]) & (offsets[place] != 0), earlier, before
            )
        table[0, place] = index_k
        table[1, place] = index_v
        table[2, place] = jnp.where(offsets[place] == 0, 1, 0)
        table[3, place] = before

    def along_z(source, target, sends, receives, step):
        pltpu.make_async_remote_copy(
            src_ref=source,
            dst_ref=target,
            send_sem=sends,
            recv_sem=receives,
            device_id=((group + step) % GROUPS, head),
            device_id_type=MESH,
        ).start()

    pools = ((kh, stage_k, pool_k, z_recv_k, POOL_K), (vh, stage_v, pool_v, z_recv_v, POOL_V))

    def landing(array, offset, rank):
        start, views = pools[array][4][offset]
        return pools[array][2].at[pl.ds(start, views), rank]

    def landed(array, offset, rank):
        return pools[array][3].at[offset - 1, rank]

    def wait_landing(array, offset, rank):
        here = landing(array, offset, rank)
        pltpu.make_async_copy(here, here, landed(array, offset, rank)).wait()

    def first_hop(array):
        source, stage = pools[array][:2]
        for rank in range(RANKS):
            for index in range(2):
                stage[index, rank] = source[exports[index] * RANKS + rank]
            for offset, step, sends in ((7, 1, 0), (1, 7, 8)):
                along_z(
                    stage.at[:, rank],
                    landing(array, offset, rank),
                    z_send.at[array, sends],
                    landed(array, offset, rank),
                    step,
                )

    def forward(array, offset, rank, choice=None):
        step = 1 if offset > 3 else 7
        target = offset - 1 if step == 1 else offset + 1
        wait_landing(array, offset, rank)
        source = landing(array, offset, rank)
        if choice is not None:
            start, pool = pools[array][4][offset][0], pools[array][2]
            chosen[choice, rank] = jnp.where(
                chosen_second[choice], pool[start + 1, rank], pool[start, rank]
            )
            source = chosen.at[pl.ds(choice, 1), rank]
        along_z(
            source,
            landing(array, target, rank),
            z_send.at[array, offset],
            landed(array, target, rank),
            step,
        )

    hops = (
        (((7, None), (1, None)), ((6, None), (2, 1)), ((5, 0),)),
        (((7, None), (1, None)), ((6, 2), (2, None)), ((3, 3),)),
    )

    def hop(array, stage, rank):
        for offset, choice in hops[array][stage]:
            forward(array, offset, rank, choice)

    def heads_of(ref, place):
        return ref[pl.ds(place * RANKS, RANKS)].reshape(LENGTH, HD)

    def own_forward(place, carry):
        k, v, q = heads_of(kh, place), heads_of(vh, place), heads_of(qh, place)
        scores = dot_nt(k, q)
        top = EXP2_SCALE * jnp.max(scores, 0, keepdims=True)
        exps = jnp.exp2(scores * EXP2_SCALE - top)
        exp_own[place] = exps
        out_own[place] = dot_nn(v.T, exps.astype(BF))
        stats[place, 0:1] = top
        stats[place, 1:2] = jnp.sum(exps, 0, keepdims=True)
        return carry

    def chain(acc, place, part):
        before = table[3, place]
        old = acc[jnp.maximum(before, 0)]
        acc[place] = part + jnp.where(before >= 0, old, 0.0)

    def far_weights(place, carry):
        off = table[2, place].astype(F32) * 1e30
        rows = pl.ds(place * RANKS, RANKS)
        q, g = heads_of(qh, place), heads_of(gh, place)
        k = pool_k[table[0, place]].reshape(LENGTH, HD)
        v = pool_v[table[1, place]].reshape(LENGTH, HD)
        scores = dot_nt(k, q)
        own_top = stats[place, 0:1]
        top = jnp.maximum(own_top, EXP2_SCALE * jnp.max(scores, 0, keepdims=True) - off)
        exps = jnp.exp2(scores * EXP2_SCALE - (top + off))
        rescale = jnp.exp2(own_top - top)
        inverse = 1.0 / (stats[place, 1:2] * rescale + jnp.sum(exps, 0, keepdims=True))
        own_factor = rescale * inverse
        weights = exps * inverse
        weights_far[place] = weights
        weights_bf = weights.astype(BF)
        out = (out_own[place] * own_factor + dot_nn(v.T, weights_bf)).astype(BF)
        oh[rows] = out.T.reshape(RANKS, ROWS, HD)
        stats[place, 2:3] = own_factor
        stats[place, 3:4] = jnp.sum(g.T.astype(F32) * out.astype(F32), 0, keepdims=True)
        chain(acc_v, place, dot_nn(weights_bf, g))
        return carry

    def far_scores(place, carry):
        q, g = heads_of(qh, place), heads_of(gh, place)
        v = pool_v[table[1, place]].reshape(LENGTH, HD)
        dscore = (weights_far[place] * (dot_nt(v, g) - stats[place, 3:4])).astype(BF)
        d_far_all[place] = dscore
        chain(acc_k, place, dot_nn(dscore, q) * SCALE)
        return carry

    def own_backward(place, carry):
        rows = pl.ds(place * RANKS, RANKS)
        k, v = heads_of(kh, place), heads_of(vh, place)
        q, g = heads_of(qh, place), heads_of(gh, place)
        far_k = pool_k[table[0, place]].reshape(LENGTH, HD)
        weights = exp_own[place] * stats[place, 2:3]
        dvh[rows] = dot_nn(weights.astype(BF), g).astype(BF).reshape(RANKS, ROWS, HD)
        dscore = (weights * (dot_nt(v, g) - stats[place, 3:4])).astype(BF)
        dkh[rows] = (dot_nn(dscore, q) * SCALE).astype(BF).reshape(RANKS, ROWS, HD)
        grad = (dot_nn(k.T, dscore) + dot_nn(far_k.T, d_far_all[place])) * SCALE
        dqh[rows] = grad.astype(BF).T.reshape(RANKS, ROWS, HD)
        return carry

    wait_heads(0, kh)
    first_hop(0)
    scatter_heads(2, q_in, qh)
    for stage in range(2):
        for rank in range(RANKS):
            hop(0, stage, rank)
    wait_heads(1, vh)
    first_hop(1)
    scatter_heads(3, g_in, gh)
    for rank in range(RANKS):
        hop(0, 2, rank)
    for rank in range(RANKS):
        hop(1, 0, rank)
    wait_heads(2, qh)
    for stage in range(1, 3):
        for rank in range(RANKS):
            hop(1, stage, rank)
            lax.fori_loop(4 * stage + rank - 4, 4 * stage + rank - 3, own_forward, 0)
    wait_heads(3, gh)
    for rank in range(RANKS):
        for array, offset in ((0, 4), (0, 3), (1, 5), (1, 4)):
            wait_landing(array, offset, rank)
    lax.fori_loop(0, PER_GROUP, far_weights, 0)

    returns = ((acc_k, ret_k, back_k, ret_recv_k), (acc_v, ret_v, back_v, ret_recv_v))
    order = (4, 3, 5, 2, 6, 1, 7)
    last = {}
    for offset in order:
        final = zero
        for place in range(PER_GROUP):
            final = jnp.where(offsets[place] == offset, place, final)
        last[offset] = final

    def send_returns(index):
        acc, ret, back, recv = returns[index]
        for rank in range(RANKS):
            for offset in order:
                ret[offset - 1, rank] = acc[last[offset], pl.ds(rank * ROWS, ROWS)].astype(BF)
                along_z(
                    ret.at[offset - 1, rank],
                    back.at[rank, OTHERS - offset],
                    ret_send.at[index],
                    recv.at[rank],
                    offset,
                )

    def gather_block(index, block, source, target):
        pltpu.make_async_remote_copy(
            src_ref=source.at[block],
            dst_ref=target.at[:, columns(head)],
            send_sem=out_send.at[index],
            recv_sem=out_recv.at[index],
            device_id=(group, block),
            device_id_type=MESH,
        ).start()

    def gather_own(index, source, target):
        pltpu.make_async_copy(
            source.at[head], target.at[:, columns(head)], out_recv.at[index]
        ).start()

    send_returns(1)
    for_peers(lambda peer: gather_block(0, peer, oh, o_out))
    gather_own(0, oh, o_out)
    lax.fori_loop(0, PER_GROUP, far_scores, 0)
    send_returns(0)
    lax.fori_loop(0, PER_GROUP, own_backward, 0)
    for_peers(lambda peer: gather_block(1, peer, dqh, dq_out))
    gather_own(1, dqh, dq_out)

    for index in (1, 0):
        for rank in range(RANKS):
            acc, ret, back, recv = returns[index]
            target = (dkh, dvh)[index]
            output = (dk_out, dv_out)[index]
            pltpu.make_async_copy(back.at[rank], back.at[rank], recv.at[rank]).wait()
            first_sum = jnp.zeros((ROWS, HD), F32)
            second_sum = jnp.zeros((ROWS, HD), F32)
            for offset in range(1, GROUPS):
                part = back[rank, offset - 1].astype(F32)
                first_sum += jnp.where(wanted[offset] == exports[0], part, 0.0)
                second_sum += jnp.where(wanted[offset] == exports[1], part, 0.0)
            for place in range(PER_GROUP):
                block = place * RANKS + rank
                extra = jnp.where(
                    place == exports[0],
                    first_sum,
                    jnp.where(place == exports[1], second_sum, 0.0),
                )
                target[block] = (target[block].astype(F32) + extra).astype(BF)

                @pl.when(block != head)
                def _():
                    gather_block(2 + index, block, target, output)

                @pl.when(block == head)
                def _():
                    gather_own(2 + index, target, output)

    for index, output in enumerate((o_out, dq_out, dk_out, dv_out)):
        pltpu.make_async_copy(output, output, out_recv.at[index]).wait()
    for index, source in enumerate((kh, vh, qh, gh)):
        blocks = source.at[pl.ds(0, HEADS - 1)]
        pltpu.make_async_copy(blocks, blocks, in_send.at[index]).wait()
        pltpu.make_async_copy(blocks, blocks, out_send.at[index]).wait()
    for array, stage in ((0, stage_k), (1, stage_v)):
        one = stage.at[pl.ds(0, 1)]
        for sends in (0, 8):
            pltpu.make_async_copy(stage, stage, z_send.at[array, sends]).wait()
        for level in hops[array]:
            for offset, choice in level:
                sent = stage if choice is None else one
                pltpu.make_async_copy(sent, sent, z_send.at[array, offset]).wait()
    for index, ret in ((0, ret_k), (1, ret_v)):
        pltpu.make_async_copy(ret, ret, ret_send.at[index]).wait()


def hand_over(*refs):
    for index in range(4):
        refs[4 + index][...] = refs[index][...]


def on_device(query_tokens, key_tokens, value_tokens, cotangent, neighbors, view_slot):
    heads_buffer = pltpu.VMEM((HEADS, ROWS, HD), BF)

    def views(count):
        return pltpu.VMEM((count, RANKS, ROWS, HD), BF)

    back_buffer = pltpu.VMEM((RANKS, OTHERS, ROWS, HD), BF)
    sum_buffer = pltpu.VMEM((PER_GROUP, LENGTH, HD), F32)
    dma = pltpu.SemaphoreType.DMA
    smem = pl.BlockSpec(memory_space=pltpu.SMEM)
    anywhere = pl.BlockSpec(memory_space=pl.ANY)
    out = jax.ShapeDtypeStruct(query_tokens.shape, BF)
    results = pl.pallas_call(
        kernel,
        out_shape=(out,) * 4,
        in_specs=[smem] * 2 + [anywhere] * 4,
        out_specs=(anywhere,) * 4,
        scratch_shapes=[heads_buffer] * 4
        + [views(2)] * 2
        + [views(len(CHOICES))]
        + [views(POOL)] * 2
        + [heads_buffer] * 4
        + [
            pltpu.VMEM((PER_GROUP, LENGTH, LENGTH), F32),
            pltpu.VMEM((PER_GROUP, HD, LENGTH), F32),
            pltpu.VMEM((PER_GROUP, 8, LENGTH), F32),
            pltpu.VMEM((PER_GROUP, LENGTH, LENGTH), F32),
            pltpu.VMEM((PER_GROUP, LENGTH, LENGTH), BF),
        ]
        + [sum_buffer] * 2
        + [views(OTHERS)] * 2
        + [back_buffer] * 2
        + [pltpu.SMEM((4, PER_GROUP), jnp.int32)]
        + [dma((4,))] * 2
        + [dma((2, 9))]
        + [dma((OTHERS, RANKS))] * 2
        + [dma((2,))]
        + [dma((RANKS,))] * 2
        + [dma((4,))] * 2,
        compiler_params=pltpu.CompilerParams(
            collective_id=0, has_side_effects=True, vmem_limit_bytes=56 << 20
        ),
    )(neighbors.T, view_slot, query_tokens, key_tokens, value_tokens, cotangent)
    block = pl.BlockSpec((ROWS // PARTS, query_tokens.shape[1]), lambda part: (part, 0))
    return pl.pallas_call(
        hand_over,
        grid=(PARTS,),
        out_shape=(out,) * 4,
        in_specs=[block] * 4,
        out_specs=(block,) * 4,
    )(*results)


def solution(mesh):
    rows = P(("view", "head"), None)
    return jax.shard_map(
        on_device,
        mesh=mesh,
        in_specs=(rows, rows, rows, rows, P(), P()),
        out_specs=(rows, rows, rows, rows),
        check_vma=False,
    )
```

```python
import functools
import math

import jax
import jax.numpy as jnp
from jax import lax
from jax.experimental import pallas as pl
from jax.experimental.pallas import tpu as pltpu
from jax.sharding import PartitionSpec as P

MESH = pl.DeviceIdType.MESH
GROUPS = 8
HEADS = 32
PER_GROUP = 8
RANKS = 4
ROWS = 128
HD = 128
LENGTH = 512
OTHERS = GROUPS - 1
PARTS = 4
SCALE = 1.0 / math.sqrt(HD)
EXP2_SCALE = math.log2(math.e) / math.sqrt(HD)
BF = jnp.bfloat16
F32 = jnp.float32


def ring_distance(step):
    return min(step, 4 - step)


PEERS = sorted(
    (
        (dy, dx, dc)
        for dy in range(4)
        for dx in range(4)
        for dc in range(2)
        if (dy, dx, dc) != (0, 0, 0)
    ),
    key=lambda step: (-ring_distance(step[0]) - ring_distance(step[1]), step),
)

POOL_K = {7: (0, 2), 6: (2, 2), 5: (4, 2), 4: (6, 1), 1: (7, 2), 2: (9, 2), 3: (11, 1)}
POOL_V = {7: (0, 2), 6: (2, 2), 5: (4, 1), 1: (5, 2), 2: (7, 2), 3: (9, 2), 4: (11, 1)}
POOL = 12
CHOICES = ((5, 1), (2, 7), (6, 1), (3, 7))


def dot_nt(a, b):
    return lax.dot_general(a, b, (((1,), (1,)), ((), ())), preferred_element_type=F32)


def dot_nn(a, b):
    return lax.dot_general(a, b, (((1,), (0,)), ((), ())), preferred_element_type=F32)


def kernel(
    neighbors, view_slot, q_in, k_in, v_in, g_in,
    o_out, dq_out, dk_out, dv_out,
    qh, kh, vh, gh,
    stage_k, stage_v, chosen, pool_k, pool_v,
    oh, dqh, dkh, dvh,
    exp_own, out_own, stats, weights_far, d_far_all,
    acc_k, acc_v, ret_k, ret_v, back_k, back_v,
    table,
    in_send, in_recv, z_send, z_recv_k, z_recv_v,
    ret_send, ret_recv_k, ret_recv_v, out_send, out_recv,
):
    group = lax.axis_index("view")
    head = lax.axis_index("head")
    row_y, col_x, core = head // 8, (head // 2) % 4, head % 2

    def for_peers(body):
        for dy, dx, dc in PEERS:
            body((((row_y + dy) % 4) * 4 + (col_x + dx) % 4) * 2 + (core + dc) % 2)

    def columns(index):
        return pl.ds(pl.multiple_of(index * HD, HD), HD)

    barrier = pltpu.get_barrier_semaphore()

    def greet(peer):
        pl.semaphore_signal(barrier, inc=1, device_id=(group, peer), device_id_type=MESH)

    for_peers(greet)
    for step in range(1, GROUPS):
        pl.semaphore_signal(
            barrier, inc=1, device_id=((group + step) % GROUPS, head), device_id_type=MESH
        )
    pl.semaphore_wait(barrier, HEADS - 1 + OTHERS)

    def scatter_heads(index, source, target):
        def send(peer):
            pltpu.make_async_remote_copy(
                src_ref=source.at[:, columns(peer)],
                dst_ref=target.at[head],
                send_sem=in_send.at[index],
                recv_sem=in_recv.at[index],
                device_id=(group, peer),
                device_id_type=MESH,
            ).start()

        for_peers(send)
        pltpu.make_async_copy(
            source.at[:, columns(head)], target.at[head], in_recv.at[index]
        ).start()

    def wait_heads(index, target):
        pltpu.make_async_copy(target, target, in_recv.at[index]).wait()

    scatter_heads(0, k_in, kh)
    scatter_heads(1, v_in, vh)

    def read_links(view, carry):
        named, lowest, highest, chosen_place, wanted = carry
        slot = view_slot[view]
        other = view_slot[neighbors[1, view]]
        slot_group, slot_place = slot >> 3, slot & 7
        other_group, other_place = other >> 3, other & 7
        own = slot_group == group
        far = slot_group != other_group
        reader = (slot_group - group) & 7
        owner = (other_group - group) & 7
        named = tuple(
            jnp.where(own & (slot_place == place), other, named[place])
            for place in range(PER_GROUP)
        )
        lowest = tuple(
            jnp.where(far & (owner == index), jnp.minimum(other_place, lowest[index]), lowest[index])
            for index in range(GROUPS)
        )
        highest = jnp.where(far & (owner == 0), jnp.maximum(other_place, highest), highest)
        chosen_place = tuple(
            jnp.where((owner == first) & (reader == second), other_place, current)
            for (first, second), current in zip(CHOICES, chosen_place)
        )
        wanted = tuple(
            jnp.where((owner == 0) & (reader == index), other_place, wanted[index])
            for index in range(GROUPS)
        )
        return named, lowest, highest, chosen_place, wanted

    zero = jnp.int32(0)
    named, lowest, highest, chosen_place, wanted = lax.fori_loop(
        0,
        PER_GROUP * GROUPS,
        read_links,
        (
            (zero,) * PER_GROUP,
            (zero + 7,) * GROUPS,
            zero,
            (zero,) * len(CHOICES),
            (zero - 1,) * GROUPS,
        ),
    )
    exports = (lowest[0], highest)
    chosen_second = tuple(
        place > lowest[owner] for (owner, _), place in zip(CHOICES, chosen_place)
    )
    offsets = tuple(((slot >> 3) - group) & 7 for slot in named)
    for place in range(PER_GROUP):
        index_k, index_v = zero, zero
        for offset in range(1, GROUPS):
            second = jnp.where((named[place] & 7) > lowest[offset], 1, 0)
            here = offsets[place] == offset
            start, views = POOL_K[offset]
            index_k = jnp.where(here, start + (second if views == 2 else 0), index_k)
            start, views = POOL_V[offset]
            index_v = jnp.where(here, start + (second if views == 2 else 0), index_v)
        before = zero - 1
        for earlier in range(place):
            before = jnp.where(
                (offsets[earlier] == offsets[place]) & (offsets[place] != 0), earlier, before
            )
        table[0, place] = index_k
        table[1, place] = index_v
        table[2, place] = jnp.where(offsets[place] == 0, 1, 0)
        table[3, place] = before

    def along_z(source, target, sends, receives, step):
        pltpu.make_async_remote_copy(
            src_ref=source,
            dst_ref=target,
            send_sem=sends,
            recv_sem=receives,
            device_id=((group + step) % GROUPS, head),
            device_id_type=MESH,
        ).start()

    pools = ((kh, stage_k, pool_k, z_recv_k, POOL_K), (vh, stage_v, pool_v, z_recv_v, POOL_V))

    def landing(array, offset, rank):
        start, views = pools[array][4][offset]
        return pools[array][2].at[pl.ds(start, views), rank]

    def landed(array, offset, rank):
        return pools[array][3].at[offset - 1, rank]

    def wait_landing(array, offset, rank):
        here = landing(array, offset, rank)
        pltpu.make_async_copy(here, here, landed(array, offset, rank)).wait()

    def first_hop(array):
        source, stage = pools[array][:2]
        for rank in range(RANKS):
            for index in range(2):
                stage[index, rank] = source[exports[index] * RANKS + rank]
            for offset, step, sends in ((7, 1, 0), (1, 7, 8)):
                along_z(
                    stage.at[:, rank],
                    landing(array, offset, rank),
                    z_send.at[array, sends],
                    landed(array, offset, rank),
                    step,
                )

    def forward(array, offset, rank, choice=None):
        step = 1 if offset > 3 else 7
        target = offset - 1 if step == 1 else offset + 1
        wait_landing(array, offset, rank)
        source = landing(array, offset, rank)
        if choice is not None:
            start, pool = pools[array][4][offset][0], pools[array][2]
            chosen[choice, rank] = jnp.where(
                chosen_second[choice], pool[start + 1, rank], pool[start, rank]
            )
            source = chosen.at[pl.ds(choice, 1), rank]
        along_z(
            source,
            landing(array, target, rank),
            z_send.at[array, offset],
            landed(array, target, rank),
            step,
        )

    hops = (
        (((7, None), (1, None)), ((6, None), (2, 1)), ((5, 0),)),
        (((7, None), (1, None)), ((6, 2), (2, None)), ((3, 3),)),
    )

    def hop(array, stage, rank):
        for offset, choice in hops[array][stage]:
            forward(array, offset, rank, choice)

    def heads_of(ref, place):
        return ref[pl.ds(place * RANKS, RANKS)].reshape(LENGTH, HD)

    def own_forward(place, carry):
        k, v, q = heads_of(kh, place), heads_of(vh, place), heads_of(qh, place)
        scores = dot_nt(k, q)
        top = EXP2_SCALE * jnp.max(scores, 0, keepdims=True)
        exps = jnp.exp2(scores * EXP2_SCALE - top)
        exp_own[place] = exps
        out_own[place] = dot_nn(v.T, exps.astype(BF))
        stats[place, 0:1] = top
        stats[place, 1:2] = jnp.sum(exps, 0, keepdims=True)
        return carry

    def chain(acc, place, part):
        before = table[3, place]
        old = acc[jnp.maximum(before, 0)]
        acc[place] = part + jnp.where(before >= 0, old, 0.0)

    def far_weights(place, carry):
        off = table[2, place].astype(F32) * 1e30
        scores = dot_nt(pool_k[table[0, place]].reshape(LENGTH, HD), heads_of(qh, place))
        own_top = stats[place, 0:1]
        top = jnp.maximum(own_top, EXP2_SCALE * jnp.max(scores, 0, keepdims=True) - off)
        exps = jnp.exp2(scores * EXP2_SCALE - (top + off))
        rescale = jnp.exp2(own_top - top)
        inverse = 1.0 / (stats[place, 1:2] * rescale + jnp.sum(exps, 0, keepdims=True))
        own_factor = rescale * inverse
        weights_far[place] = exps * inverse
        stats[place, 2:3] = own_factor
        return carry

    def far_values(place, carry):
        rows = pl.ds(place * RANKS, RANKS)
        g = heads_of(gh, place)
        v = pool_v[table[1, place]].reshape(LENGTH, HD)
        weights_bf = weights_far[place].astype(BF)
        out = (out_own[place] * stats[place, 2:3] + dot_nn(v.T, weights_bf)).astype(BF)
        oh[rows] = out.T.reshape(RANKS, ROWS, HD)
        stats[place, 3:4] = jnp.sum(g.T.astype(F32) * out.astype(F32), 0, keepdims=True)
        chain(acc_v, place, dot_nn(weights_bf, g))
        return carry

    def far_scores(place, carry):
        q, g = heads_of(qh, place), heads_of(gh, place)
        v = pool_v[table[1, place]].reshape(LENGTH, HD)
        dscore = (weights_far[place] * (dot_nt(v, g) - stats[place, 3:4])).astype(BF)
        d_far_all[place] = dscore
        chain(acc_k, place, dot_nn(dscore, q) * SCALE)
        return carry

    def own_backward(place, carry):
        rows = pl.ds(place * RANKS, RANKS)
        k, v = heads_of(kh, place), heads_of(vh, place)
        q, g = heads_of(qh, place), heads_of(gh, place)
        far_k = pool_k[table[0, place]].reshape(LENGTH, HD)
        weights = exp_own[place] * stats[place, 2:3]
        dvh[rows] = dot_nn(weights.astype(BF), g).astype(BF).reshape(RANKS, ROWS, HD)
        dscore = (weights * (dot_nt(v, g) - stats[place, 3:4])).astype(BF)
        dkh[rows] = (dot_nn(dscore, q) * SCALE).astype(BF).reshape(RANKS, ROWS, HD)
        grad = (dot_nn(k.T, dscore) + dot_nn(far_k.T, d_far_all[place])) * SCALE
        dqh[rows] = grad.astype(BF).T.reshape(RANKS, ROWS, HD)
        return carry

    wait_heads(0, kh)
    first_hop(0)
    scatter_heads(2, q_in, qh)
    for stage in range(2):
        for rank in range(RANKS):
            hop(0, stage, rank)
    wait_heads(1, vh)
    first_hop(1)
    scatter_heads(3, g_in, gh)
    for rank in range(RANKS):
        hop(0, 2, rank)
    for rank in range(RANKS):
        hop(1, 0, rank)
    wait_heads(2, qh)
    for rank in range(RANKS):
        hop(1, 1, rank)
        lax.fori_loop(2 * rank, 2 * rank + 2, own_forward, 0, unroll=2)
    for rank in range(RANKS):
        wait_landing(0, 4, rank)
        wait_landing(0, 3, rank)
    for rank in range(RANKS):
        hop(1, 2, rank)
        lax.fori_loop(2 * rank, 2 * rank + 2, far_weights, 0, unroll=2)
    wait_heads(3, gh)
    for rank in range(RANKS):
        wait_landing(1, 5, rank)
        wait_landing(1, 4, rank)
    lax.fori_loop(0, PER_GROUP, far_values, 0, unroll=2)

    returns = ((acc_k, ret_k, back_k, ret_recv_k), (acc_v, ret_v, back_v, ret_recv_v))
    order = (4, 3, 5, 2, 6, 1, 7)
    last = {}
    for offset in order:
        final = zero
        for place in range(PER_GROUP):
            final = jnp.where(offsets[place] == offset, place, final)
        last[offset] = final

    def send_returns(index):
        acc, ret, back, recv = returns[index]
        for rank in range(RANKS):
            for offset in order:
                ret[offset - 1, rank] = acc[last[offset], pl.ds(rank * ROWS, ROWS)].astype(BF)
                along_z(
                    ret.at[offset - 1, rank],
                    back.at[rank, OTHERS - offset],
                    ret_send.at[index],
                    recv.at[rank],
                    offset,
                )

    def gather_block(index, block, source, target):
        pltpu.make_async_remote_copy(
            src_ref=source.at[block],
            dst_ref=target.at[:, columns(head)],
            send_sem=out_send.at[index],
            recv_sem=out_recv.at[index],
            device_id=(group, block),
            device_id_type=MESH,
        ).start()

    def gather_own(index, source, target):
        pltpu.make_async_copy(
            source.at[head], target.at[:, columns(head)], out_recv.at[index]
        ).start()

    send_returns(1)
    for_peers(lambda peer: gather_block(0, peer, oh, o_out))
    gather_own(0, oh, o_out)
    lax.fori_loop(0, PER_GROUP, far_scores, 0, unroll=2)
    send_returns(0)
    lax.fori_loop(0, PER_GROUP, own_backward, 0, unroll=2)
    for_peers(lambda peer: gather_block(1, peer, dqh, dq_out))
    gather_own(1, dqh, dq_out)

    for index in (1, 0):
        for rank in range(RANKS):
            acc, ret, back, recv = returns[index]
            target = (dkh, dvh)[index]
            output = (dk_out, dv_out)[index]
            pltpu.make_async_copy(back.at[rank], back.at[rank], recv.at[rank]).wait()
            first_sum = jnp.zeros((ROWS, HD), F32)
            second_sum = jnp.zeros((ROWS, HD), F32)
            for offset in range(1, GROUPS):
                part = back[rank, offset - 1].astype(F32)
                first_sum += jnp.where(wanted[offset] == exports[0], part, 0.0)
                second_sum += jnp.where(wanted[offset] == exports[1], part, 0.0)
            for place in range(PER_GROUP):
                block = place * RANKS + rank
                extra = jnp.where(
                    place == exports[0],
                    first_sum,
                    jnp.where(place == exports[1], second_sum, 0.0),
                )
                target[block] = (target[block].astype(F32) + extra).astype(BF)

                @pl.when(block != head)
                def _():
                    gather_block(2 + index, block, target, output)

                @pl.when(block == head)
                def _():
                    gather_own(2 + index, target, output)

    for index, output in enumerate((o_out, dq_out, dk_out, dv_out)):
        pltpu.make_async_copy(output, output, out_recv.at[index]).wait()
    for index, source in enumerate((kh, vh, qh, gh)):
        blocks = source.at[pl.ds(0, HEADS - 1)]
        pltpu.make_async_copy(blocks, blocks, in_send.at[index]).wait()
        pltpu.make_async_copy(blocks, blocks, out_send.at[index]).wait()
    for array, stage in ((0, stage_k), (1, stage_v)):
        one = stage.at[pl.ds(0, 1)]
        for sends in (0, 8):
            pltpu.make_async_copy(stage, stage, z_send.at[array, sends]).wait()
        for level in hops[array]:
            for offset, choice in level:
                sent = stage if choice is None else one
                pltpu.make_async_copy(sent, sent, z_send.at[array, offset]).wait()
    for index, ret in ((0, ret_k), (1, ret_v)):
        pltpu.make_async_copy(ret, ret, ret_send.at[index]).wait()


def hand_over(*refs):
    for index in range(4):
        refs[4 + index][...] = refs[index][...]


def on_device(query_tokens, key_tokens, value_tokens, cotangent, neighbors, view_slot):
    heads_buffer = pltpu.VMEM((HEADS, ROWS, HD), BF)

    def views(count):
        return pltpu.VMEM((count, RANKS, ROWS, HD), BF)

    back_buffer = pltpu.VMEM((RANKS, OTHERS, ROWS, HD), BF)
    sum_buffer = pltpu.VMEM((PER_GROUP, LENGTH, HD), F32)
    dma = pltpu.SemaphoreType.DMA
    smem = pl.BlockSpec(memory_space=pltpu.SMEM)
    anywhere = pl.BlockSpec(memory_space=pl.ANY)
    out = jax.ShapeDtypeStruct(query_tokens.shape, BF)
    results = pl.pallas_call(
        kernel,
        out_shape=(out,) * 4,
        in_specs=[smem] * 2 + [anywhere] * 4,
        out_specs=(anywhere,) * 4,
        scratch_shapes=[heads_buffer] * 4
        + [views(2)] * 2
        + [views(len(CHOICES))]
        + [views(POOL)] * 2
        + [heads_buffer] * 4
        + [
            pltpu.VMEM((PER_GROUP, LENGTH, LENGTH), F32),
            pltpu.VMEM((PER_GROUP, HD, LENGTH), F32),
            pltpu.VMEM((PER_GROUP, 8, LENGTH), F32),
            pltpu.VMEM((PER_GROUP, LENGTH, LENGTH), F32),
            pltpu.VMEM((PER_GROUP, LENGTH, LENGTH), BF),
        ]
        + [sum_buffer] * 2
        + [views(OTHERS)] * 2
        + [back_buffer] * 2
        + [pltpu.SMEM((4, PER_GROUP), jnp.int32)]
        + [dma((4,))] * 2
        + [dma((2, 9))]
        + [dma((OTHERS, RANKS))] * 2
        + [dma((2,))]
        + [dma((RANKS,))] * 2
        + [dma((4,))] * 2,
        compiler_params=pltpu.CompilerParams(
            collective_id=0, has_side_effects=True, vmem_limit_bytes=56 << 20
        ),
    )(neighbors.T, view_slot, query_tokens, key_tokens, value_tokens, cotangent)
    block = pl.BlockSpec((ROWS // PARTS, query_tokens.shape[1]), lambda part: (part, 0))
    return pl.pallas_call(
        hand_over,
        grid=(PARTS,),
        out_shape=(out,) * 4,
        in_specs=[block] * 4,
        out_specs=(block,) * 4,
    )(*results)


def solution(mesh):
    rows = P(("view", "head"), None)
    return jax.shard_map(
        on_device,
        mesh=mesh,
        in_specs=(rows, rows, rows, rows, P(), P()),
        out_specs=(rows, rows, rows, rows),
        check_vma=False,
    )
```

```python
import functools
import math

import jax
import jax.numpy as jnp
from jax import lax
from jax.experimental import pallas as pl
from jax.experimental.pallas import tpu as pltpu
from jax.sharding import PartitionSpec as P

MESH = pl.DeviceIdType.MESH
GROUPS = 8
HEADS = 32
PER_GROUP = 8
RANKS = 4
ROWS = 128
HD = 128
LENGTH = 512
OTHERS = GROUPS - 1
PARTS = 4
SCALE = 1.0 / math.sqrt(HD)
EXP2_SCALE = math.log2(math.e) / math.sqrt(HD)
BF = jnp.bfloat16
F32 = jnp.float32


def ring_distance(step):
    return min(step, 4 - step)


PEERS = sorted(
    (
        (dy, dx, dc)
        for dy in range(4)
        for dx in range(4)
        for dc in range(2)
        if (dy, dx, dc) != (0, 0, 0)
    ),
    key=lambda step: (-ring_distance(step[0]) - ring_distance(step[1]), step),
)

POOL_K = {7: (0, 2), 6: (2, 2), 5: (4, 2), 4: (6, 1), 1: (7, 2), 2: (9, 2), 3: (11, 1)}
POOL_V = {7: (0, 2), 6: (2, 2), 5: (4, 1), 1: (5, 2), 2: (7, 2), 3: (9, 2), 4: (11, 1)}
POOL = 12
CHOICES = ((5, 1), (2, 7), (6, 1), (3, 7))


def dot_nt(a, b):
    return lax.dot_general(a, b, (((1,), (1,)), ((), ())), preferred_element_type=F32)


def dot_nn(a, b):
    return lax.dot_general(a, b, (((1,), (0,)), ((), ())), preferred_element_type=F32)


def kernel(
    neighbors, view_slot, q_in, k_in, v_in, g_in,
    o_out, dq_out, dk_out, dv_out,
    qh, kh, vh, gh,
    stage_k, stage_v, chosen, pool_k, pool_v,
    oh, dqh, dkh, dvh,
    exp_own, out_own, stats, weights_far, d_far_all,
    acc_k, acc_v, ret_k, ret_v, back_k, back_v,
    table,
    in_send, in_recv, z_send, z_recv_k, z_recv_v,
    ret_send, ret_recv_k, ret_recv_v, out_send, out_recv,
):
    group = lax.axis_index("view")
    head = lax.axis_index("head")
    row_y, col_x, core = head // 8, (head // 2) % 4, head % 2

    def for_peers(body):
        for dy, dx, dc in PEERS:
            body((((row_y + dy) % 4) * 4 + (col_x + dx) % 4) * 2 + (core + dc) % 2)

    def columns(index):
        return pl.ds(pl.multiple_of(index * HD, HD), HD)

    barrier = pltpu.get_barrier_semaphore()

    def greet(peer):
        pl.semaphore_signal(barrier, inc=1, device_id=(group, peer), device_id_type=MESH)

    for_peers(greet)
    for step in range(1, GROUPS):
        pl.semaphore_signal(
            barrier, inc=1, device_id=((group + step) % GROUPS, head), device_id_type=MESH
        )
    pl.semaphore_wait(barrier, HEADS - 1 + OTHERS)

    def scatter_heads(index, source, target):
        def send(peer):
            pltpu.make_async_remote_copy(
                src_ref=source.at[:, columns(peer)],
                dst_ref=target.at[head],
                send_sem=in_send.at[index],
                recv_sem=in_recv.at[index],
                device_id=(group, peer),
                device_id_type=MESH,
            ).start()

        for_peers(send)
        pltpu.make_async_copy(
            source.at[:, columns(head)], target.at[head], in_recv.at[index]
        ).start()

    def wait_heads(index, target):
        pltpu.make_async_copy(target, target, in_recv.at[index]).wait()

    scatter_heads(0, k_in, kh)
    scatter_heads(1, v_in, vh)

    def read_links(view, carry):
        named, lowest, highest, chosen_place, wanted = carry
        slot = view_slot[view]
        other = view_slot[neighbors[1, view]]
        slot_group, slot_place = slot >> 3, slot & 7
        other_group, other_place = other >> 3, other & 7
        own = slot_group == group
        far = slot_group != other_group
        reader = (slot_group - group) & 7
        owner = (other_group - group) & 7
        named = tuple(
            jnp.where(own & (slot_place == place), other, named[place])
            for place in range(PER_GROUP)
        )
        lowest = tuple(
            jnp.where(far & (owner == index), jnp.minimum(other_place, lowest[index]), lowest[index])
            for index in range(GROUPS)
        )
        highest = jnp.where(far & (owner == 0), jnp.maximum(other_place, highest), highest)
        chosen_place = tuple(
            jnp.where((owner == first) & (reader == second), other_place, current)
            for (first, second), current in zip(CHOICES, chosen_place)
        )
        wanted = tuple(
            jnp.where((owner == 0) & (reader == index), other_place, wanted[index])
            for index in range(GROUPS)
        )
        return named, lowest, highest, chosen_place, wanted

    zero = jnp.int32(0)
    named, lowest, highest, chosen_place, wanted = lax.fori_loop(
        0,
        PER_GROUP * GROUPS,
        read_links,
        (
            (zero,) * PER_GROUP,
            (zero + 7,) * GROUPS,
            zero,
            (zero,) * len(CHOICES),
            (zero - 1,) * GROUPS,
        ),
    )
    exports = (lowest[0], highest)
    chosen_second = tuple(
        place > lowest[owner] for (owner, _), place in zip(CHOICES, chosen_place)
    )
    offsets = tuple(((slot >> 3) - group) & 7 for slot in named)
    for place in range(PER_GROUP):
        index_k, index_v = zero, zero
        for offset in range(1, GROUPS):
            second = jnp.where((named[place] & 7) > lowest[offset], 1, 0)
            here = offsets[place] == offset
            start, views = POOL_K[offset]
            index_k = jnp.where(here, start + (second if views == 2 else 0), index_k)
            start, views = POOL_V[offset]
            index_v = jnp.where(here, start + (second if views == 2 else 0), index_v)
        before = zero - 1
        for earlier in range(place):
            before = jnp.where(
                (offsets[earlier] == offsets[place]) & (offsets[place] != 0), earlier, before
            )
        table[0, place] = index_k
        table[1, place] = index_v
        table[2, place] = jnp.where(offsets[place] == 0, 1, 0)
        table[3, place] = before

    def along_z(source, target, sends, receives, step):
        pltpu.make_async_remote_copy(
            src_ref=source,
            dst_ref=target,
            send_sem=sends,
            recv_sem=receives,
            device_id=((group + step) % GROUPS, head),
            device_id_type=MESH,
        ).start()

    pools = ((kh, stage_k, pool_k, z_recv_k, POOL_K), (vh, stage_v, pool_v, z_recv_v, POOL_V))

    def landing(array, offset, rank):
        start, views = pools[array][4][offset]
        return pools[array][2].at[pl.ds(start, views), rank]

    def landed(array, offset, rank):
        return pools[array][3].at[offset - 1, rank]

    def wait_landing(array, offset, rank):
        here = landing(array, offset, rank)
        pltpu.make_async_copy(here, here, landed(array, offset, rank)).wait()

    def first_hop(array):
        source, stage = pools[array][:2]
        for rank in range(RANKS):
            for index in range(2):
                stage[index, rank] = source[exports[index] * RANKS + rank]
            for offset, step, sends in ((7, 1, 0), (1, 7, 8)):
                along_z(
                    stage.at[:, rank],
                    landing(array, offset, rank),
                    z_send.at[array, sends],
                    landed(array, offset, rank),
                    step,
                )

    def forward(array, offset, rank, choice=None):
        step = 1 if offset > 3 else 7
        target = offset - 1 if step == 1 else offset + 1
        wait_landing(array, offset, rank)
        source = landing(array, offset, rank)
        if choice is not None:
            start, pool = pools[array][4][offset][0], pools[array][2]
            chosen[choice, rank] = jnp.where(
                chosen_second[choice], pool[start + 1, rank], pool[start, rank]
            )
            source = chosen.at[pl.ds(choice, 1), rank]
        along_z(
            source,
            landing(array, target, rank),
            z_send.at[array, offset],
            landed(array, target, rank),
            step,
        )

    hops = (
        (((7, None), (1, None)), ((6, None), (2, 1)), ((5, 0),)),
        (((7, None), (1, None)), ((6, 2), (2, None)), ((3, 3),)),
    )

    def hop(array, stage, rank):
        for offset, choice in hops[array][stage]:
            forward(array, offset, rank, choice)

    def heads_of(ref, place):
        return ref[pl.ds(place * RANKS, RANKS)].reshape(LENGTH, HD)

    def own_forward(place, carry):
        k, v, q = heads_of(kh, place), heads_of(vh, place), heads_of(qh, place)
        scores = dot_nt(k, q)
        top = EXP2_SCALE * jnp.max(scores, 0, keepdims=True)
        exps = jnp.exp2(scores * EXP2_SCALE - top)
        exp_own[place] = exps
        out_own[place] = dot_nn(v.T, exps.astype(BF))
        stats[place, 0:1] = top
        stats[place, 1:2] = jnp.sum(exps, 0, keepdims=True)
        return carry

    def chain(acc, place, part):
        before = table[3, place]
        old = acc[jnp.maximum(before, 0)]
        acc[place] = part + jnp.where(before >= 0, old, 0.0)

    def far_weights(place, carry):
        off = table[2, place].astype(F32) * 1e30
        scores = dot_nt(pool_k[table[0, place]].reshape(LENGTH, HD), heads_of(qh, place))
        own_top = stats[place, 0:1]
        top = jnp.maximum(own_top, EXP2_SCALE * jnp.max(scores, 0, keepdims=True) - off)
        exps = jnp.exp2(scores * EXP2_SCALE - (top + off))
        rescale = jnp.exp2(own_top - top)
        inverse = 1.0 / (stats[place, 1:2] * rescale + jnp.sum(exps, 0, keepdims=True))
        own_factor = rescale * inverse
        weights_far[place] = exps * inverse
        stats[place, 2:3] = own_factor
        return carry

    def far_values(place, carry):
        rows = pl.ds(place * RANKS, RANKS)
        g = heads_of(gh, place)
        v = pool_v[table[1, place]].reshape(LENGTH, HD)
        weights_bf = weights_far[place].astype(BF)
        out = (out_own[place] * stats[place, 2:3] + dot_nn(v.T, weights_bf)).astype(BF)
        oh[rows] = out.T.reshape(RANKS, ROWS, HD)
        stats[place, 3:4] = jnp.sum(g.T.astype(F32) * out.astype(F32), 0, keepdims=True)
        chain(acc_v, place, dot_nn(weights_bf, g))
        return carry

    def far_scores(place, carry):
        q, g = heads_of(qh, place), heads_of(gh, place)
        v = pool_v[table[1, place]].reshape(LENGTH, HD)
        dscore = (weights_far[place] * (dot_nt(v, g) - stats[place, 3:4])).astype(BF)
        d_far_all[place] = dscore
        chain(acc_k, place, dot_nn(dscore, q) * SCALE)
        return carry

    def own_backward(place, carry):
        rows = pl.ds(place * RANKS, RANKS)
        k, v = heads_of(kh, place), heads_of(vh, place)
        q, g = heads_of(qh, place), heads_of(gh, place)
        far_k = pool_k[table[0, place]].reshape(LENGTH, HD)
        weights = exp_own[place] * stats[place, 2:3]
        dvh[rows] = dot_nn(weights.astype(BF), g).astype(BF).reshape(RANKS, ROWS, HD)
        dscore = (weights * (dot_nt(v, g) - stats[place, 3:4])).astype(BF)
        dkh[rows] = (dot_nn(dscore, q) * SCALE).astype(BF).reshape(RANKS, ROWS, HD)
        grad = (dot_nn(k.T, dscore) + dot_nn(far_k.T, d_far_all[place])) * SCALE
        dqh[rows] = grad.astype(BF).T.reshape(RANKS, ROWS, HD)
        return carry

    wait_heads(0, kh)
    first_hop(0)
    scatter_heads(2, q_in, qh)
    for stage in range(2):
        for rank in range(RANKS):
            hop(0, stage, rank)
    wait_heads(1, vh)
    first_hop(1)
    scatter_heads(3, g_in, gh)
    for rank in range(RANKS):
        hop(0, 2, rank)
    for rank in range(RANKS):
        hop(1, 0, rank)
    wait_heads(2, qh)
    for rank in range(RANKS):
        hop(1, 1, rank)
        lax.fori_loop(2 * rank, 2 * rank + 2, own_forward, 0, unroll=2)
    for rank in range(RANKS):
        wait_landing(0, 4, rank)
        wait_landing(0, 3, rank)
    for rank in range(RANKS):
        hop(1, 2, rank)
        lax.fori_loop(2 * rank, 2 * rank + 2, far_weights, 0, unroll=2)
    wait_heads(3, gh)
    for rank in range(RANKS):
        wait_landing(1, 5, rank)
        wait_landing(1, 4, rank)
    lax.fori_loop(0, PER_GROUP, far_values, 0, unroll=4)

    returns = ((acc_k, ret_k, back_k, ret_recv_k), (acc_v, ret_v, back_v, ret_recv_v))
    order = (4, 3, 5, 2, 6, 1, 7)
    last = {}
    for offset in order:
        final = zero
        for place in range(PER_GROUP):
            final = jnp.where(offsets[place] == offset, place, final)
        last[offset] = final

    def send_returns(index):
        acc, ret, back, recv = returns[index]
        for rank in range(RANKS):
            for offset in order:
                ret[offset - 1, rank] = acc[last[offset], pl.ds(rank * ROWS, ROWS)].astype(BF)
                along_z(
                    ret.at[offset - 1, rank],
                    back.at[rank, OTHERS - offset],
                    ret_send.at[index],
                    recv.at[rank],
                    offset,
                )

    def gather_block(index, block, source, target):
        pltpu.make_async_remote_copy(
            src_ref=source.at[block],
            dst_ref=target.at[:, columns(head)],
            send_sem=out_send.at[index],
            recv_sem=out_recv.at[index],
            device_id=(group, block),
            device_id_type=MESH,
        ).start()

    def gather_own(index, source, target):
        pltpu.make_async_copy(
            source.at[head], target.at[:, columns(head)], out_recv.at[index]
        ).start()

    send_returns(1)
    for_peers(lambda peer: gather_block(0, peer, oh, o_out))
    gather_own(0, oh, o_out)
    lax.fori_loop(0, PER_GROUP, far_scores, 0, unroll=2)
    send_returns(0)
    def own_backward_pair(pair, carry):
        for view in range(2):
            own_backward(2 * pair + view, carry)
        for index in range(2 * RANKS):
            block = 2 * RANKS * pair + index

            @pl.when(block != head)
            def _():
                gather_block(1, block, dqh, dq_out)

            @pl.when(block == head)
            def _():
                gather_own(1, dqh, dq_out)

        return carry

    lax.fori_loop(0, PER_GROUP // 2, own_backward_pair, 0)

    for index in (1, 0):
        for rank in range(RANKS):
            acc, ret, back, recv = returns[index]
            target = (dkh, dvh)[index]
            output = (dk_out, dv_out)[index]
            pltpu.make_async_copy(back.at[rank], back.at[rank], recv.at[rank]).wait()
            first_sum = jnp.zeros((ROWS, HD), F32)
            second_sum = jnp.zeros((ROWS, HD), F32)
            for offset in range(1, GROUPS):
                part = back[rank, offset - 1].astype(F32)
                first_sum += jnp.where(wanted[offset] == exports[0], part, 0.0)
                second_sum += jnp.where(wanted[offset] == exports[1], part, 0.0)
            for place in range(PER_GROUP):
                block = place * RANKS + rank
                extra = jnp.where(
                    place == exports[0],
                    first_sum,
                    jnp.where(place == exports[1], second_sum, 0.0),
                )
                target[block] = (target[block].astype(F32) + extra).astype(BF)

                @pl.when(block != head)
                def _():
                    gather_block(2 + index, block, target, output)

                @pl.when(block == head)
                def _():
                    gather_own(2 + index, target, output)

    for index, output in enumerate((o_out, dq_out, dk_out, dv_out)):
        pltpu.make_async_copy(output, output, out_recv.at[index]).wait()
    for index, source in enumerate((kh, vh, qh, gh)):
        blocks = source.at[pl.ds(0, HEADS - 1)]
        pltpu.make_async_copy(blocks, blocks, in_send.at[index]).wait()
        pltpu.make_async_copy(blocks, blocks, out_send.at[index]).wait()
    for array, stage in ((0, stage_k), (1, stage_v)):
        one = stage.at[pl.ds(0, 1)]
        for sends in (0, 8):
            pltpu.make_async_copy(stage, stage, z_send.at[array, sends]).wait()
        for level in hops[array]:
            for offset, choice in level:
                sent = stage if choice is None else one
                pltpu.make_async_copy(sent, sent, z_send.at[array, offset]).wait()
    for index, ret in ((0, ret_k), (1, ret_v)):
        pltpu.make_async_copy(ret, ret, ret_send.at[index]).wait()


def hand_over(*refs):
    for index in range(4):
        refs[4 + index][...] = refs[index][...]


def on_device(query_tokens, key_tokens, value_tokens, cotangent, neighbors, view_slot):
    heads_buffer = pltpu.VMEM((HEADS, ROWS, HD), BF)

    def views(count):
        return pltpu.VMEM((count, RANKS, ROWS, HD), BF)

    back_buffer = pltpu.VMEM((RANKS, OTHERS, ROWS, HD), BF)
    sum_buffer = pltpu.VMEM((PER_GROUP, LENGTH, HD), F32)
    dma = pltpu.SemaphoreType.DMA
    smem = pl.BlockSpec(memory_space=pltpu.SMEM)
    anywhere = pl.BlockSpec(memory_space=pl.ANY)
    out = jax.ShapeDtypeStruct(query_tokens.shape, BF)
    results = pl.pallas_call(
        kernel,
        out_shape=(out,) * 4,
        in_specs=[smem] * 2 + [anywhere] * 4,
        out_specs=(anywhere,) * 4,
        scratch_shapes=[heads_buffer] * 4
        + [views(2)] * 2
        + [views(len(CHOICES))]
        + [views(POOL)] * 2
        + [heads_buffer] * 4
        + [
            pltpu.VMEM((PER_GROUP, LENGTH, LENGTH), F32),
            pltpu.VMEM((PER_GROUP, HD, LENGTH), F32),
            pltpu.VMEM((PER_GROUP, 8, LENGTH), F32),
            pltpu.VMEM((PER_GROUP, LENGTH, LENGTH), F32),
            pltpu.VMEM((PER_GROUP, LENGTH, LENGTH), BF),
        ]
        + [sum_buffer] * 2
        + [views(OTHERS)] * 2
        + [back_buffer] * 2
        + [pltpu.SMEM((4, PER_GROUP), jnp.int32)]
        + [dma((4,))] * 2
        + [dma((2, 9))]
        + [dma((OTHERS, RANKS))] * 2
        + [dma((2,))]
        + [dma((RANKS,))] * 2
        + [dma((4,))] * 2,
        compiler_params=pltpu.CompilerParams(
            collective_id=0, has_side_effects=True, vmem_limit_bytes=56 << 20
        ),
    )(neighbors.T, view_slot, query_tokens, key_tokens, value_tokens, cotangent)
    block = pl.BlockSpec((ROWS // PARTS, query_tokens.shape[1]), lambda part: (part, 0))
    return pl.pallas_call(
        hand_over,
        grid=(PARTS,),
        out_shape=(out,) * 4,
        in_specs=[block] * 4,
        out_specs=(block,) * 4,
    )(*results)


def solution(mesh):
    rows = P(("view", "head"), None)
    return jax.shard_map(
        on_device,
        mesh=mesh,
        in_specs=(rows, rows, rows, rows, P(), P()),
        out_specs=(rows, rows, rows, rows),
        check_vma=False,
    )
```
